512 devices in a mesh: seq: 16 (over x, z_lo), res: 32 (over z_hi, y, core).
Axes of the slice: x: 4, y: 8, z: 8 (z_hi: 2, z_lo: 4; z = z_hi * 4 + z_lo), core: 2. Of those that a mesh axis runs over, the one named last changes fastest.
Arguments:
- alignment: bfloat16 [1024, 256, 256], P(('seq', 'res')), may hold values from -6 to 6
- layer_norm_gain: float32 [256], replicated, may hold values from 0.1 to 1.9
- layer_norm_bias: float32 [256], replicated, may hold values from -0.6 to 0.6
- left_projection_weight: bfloat16 [256, 32], replicated, may hold values from -0.375 to 0.375
- left_bias: float32 [32], replicated, may hold values from -0.6 to 0.6
- right_projection_weight: bfloat16 [256, 32], replicated, may hold values from -0.375 to 0.375
- right_bias: float32 [32], replicated, may hold values from -0.6 to 0.6
- out_weight: bfloat16 [1024, 128], replicated, may hold values from -6 to 6
- out_bias: float32 [128], replicated, may hold values from -3 to 3
Outputs:
- pair_update: bfloat16 [256, 256, 128], P('res', 'seq')
The draws below stay inside these ranges and needn't reach their ends.
All inputs are finite; a program needn't handle non-finite values.
Results may differ from the reference program's by a relative error of at most 0.022.
Values may be sent and summed in bfloat16 or wider, within the bound.
A program may use at most 64 MiB of HBM per device.

```python
import jax
import jax.numpy as jnp
from jax import lax

ALIGN_CHANNELS = 256
OUTER_CHANNELS = 32
PAIR_CH = 128
SEQ_DEV = 64
RES_DEV = 8
SEQUENCE_COUNT = 1024
RESIDUE_COUNT = 256
N_SEQ = 16
N_RES = 32


def shard_levels(stream_key, shape, split, low, high):
    factor_of, own = 1.0, jax.random.fold_in(stream_key, 6)
    for axis_at, shards_of in split:
        draws = jnp.exp(jax.random.uniform(jax.random.fold_in(own, axis_at), (shards_of,), jnp.float32, low / len(split), high / len(split)))
        factor_of = factor_of * jnp.repeat(draws, shape[axis_at] // shards_of).reshape([-1 if axis == axis_at else 1 for axis in range(len(shape))])
    return factor_of


def noise(rng, extent, deviation, limit, cuts=(), kind=jnp.bfloat16):
    drawn = jax.random.normal(rng, extent, jnp.float32) * deviation
    if len(cuts) > 0:
        drawn = shard_levels(rng, extent, cuts, -0.22, 0.18) * drawn
    return jnp.clip(drawn, min=-limit, max=limit).astype(kind)


def setup_inputs(seed: int = 0) -> dict:
    keys = jax.random.split(jax.random.key(seed), 10)
    alignment = noise(keys[0], (SEQUENCE_COUNT, RESIDUE_COUNT, ALIGN_CHANNELS), 1.0, 6.0, ((0, 512),))
    layer_norm_gain = jnp.clip(1.0 + 0.18 * jax.random.normal(keys[1], (ALIGN_CHANNELS,), jnp.float32), 0.1, 1.9)
    layer_norm_bias = noise(keys[2], (ALIGN_CHANNELS,), 0.1, 0.6, (), jnp.float32)
    left_projection_weight = noise(keys[3], (ALIGN_CHANNELS, OUTER_CHANNELS), ALIGN_CHANNELS ** -0.5, 0.375)
    left_bias = noise(keys[4], (OUTER_CHANNELS,), 0.1, 0.6, (), jnp.float32)
    right_projection_weight = noise(keys[5], (ALIGN_CHANNELS, OUTER_CHANNELS), ALIGN_CHANNELS ** -0.5, 0.375)
    right_bias = noise(keys[6], (OUTER_CHANNELS,), 0.1, 0.6, (), jnp.float32)
    out_weight = noise(keys[7], (OUTER_CHANNELS * OUTER_CHANNELS, PAIR_CH), 1.0, 6.0)
    out_bias = noise(keys[8], (PAIR_CH,), 0.5, 3.0, (), jnp.float32)
    return {"alignment": alignment, "layer_norm_gain": layer_norm_gain, "layer_norm_bias": layer_norm_bias, "left_projection_weight": left_projection_weight, "left_bias": left_bias, "right_projection_weight": right_projection_weight, "right_bias": right_bias, "out_weight": out_weight, "out_bias": out_bias}


def normalize_project(alignment, layer_norm_gain, layer_norm_bias, weight, bias):
    values = alignment.astype(jnp.float32)
    centre = lax.optimization_barrier(jnp.mean(values, axis=-1, keepdims=True))
    spread = lax.optimization_barrier(jnp.mean((values - centre) ** 2, axis=-1, keepdims=True))
    normed = ((values - centre) * lax.rsqrt(spread + 1e-05) * layer_norm_gain + layer_norm_bias).astype(jnp.bfloat16)
    flat = normed.reshape(-1, normed.shape[-1])
    result = jnp.dot(flat, weight, preferred_element_type=jnp.float32) + bias
    return result.astype(jnp.bfloat16).reshape(normed.shape[:-1] + (weight.shape[1],))

def reference(alignment, layer_norm_gain, layer_norm_bias, left_projection_weight, left_bias, right_projection_weight, right_bias, out_weight, out_bias):
    left_proj = normalize_project(alignment, layer_norm_gain, layer_norm_bias, left_projection_weight, left_bias)
    right_proj = normalize_project(alignment, layer_norm_gain, layer_norm_bias, right_projection_weight, right_bias)
    seq_total = alignment.shape[0]
    res_total = alignment.shape[1]
    hidden_width = left_projection_weight.shape[1]
    left_groups = left_proj.reshape(N_SEQ, SEQ_DEV, res_total, hidden_width)
    right_groups = right_proj.reshape(N_SEQ, SEQ_DEV, res_total, hidden_width)

    def one_block(block_index):
        left_rows = lax.dynamic_slice_in_dim(left_groups, (block_index * RES_DEV).astype(jnp.int32), RES_DEV, 2)

        def add_group(running, pair_in):
            left_part, right_part = pair_in
            outer_block = jnp.einsum('sic,sjd->ijcd', left_part.astype(jnp.float32), right_part.astype(jnp.float32)) / float(seq_total)
            outer_block = outer_block.astype(jnp.bfloat16).reshape(RES_DEV * res_total, hidden_width * hidden_width)
            term_block = jnp.dot(outer_block, out_weight, preferred_element_type=jnp.float32)
            return (running + term_block.reshape(RES_DEV, res_total, -1), None)
        start_value = jnp.zeros((RES_DEV, res_total, out_weight.shape[1]), jnp.float32)
        running, unused = lax.scan(add_group, start_value, (left_rows, right_groups))
        return (running + out_bias).astype(jnp.bfloat16)
    blocks = lax.map(one_block, jnp.arange(N_RES, dtype=jnp.int32))
    return blocks.reshape(res_total, res_total, out_weight.shape[1])
```

```python
import functools

import jax
import jax.numpy as jnp
from jax import lax
from jax.experimental import pallas as pl
from jax.experimental.pallas import tpu as pltpu
from jax.sharding import PartitionSpec as P

MESH = pl.DeviceIdType.MESH
F32 = jnp.float32
BF16 = jnp.bfloat16
NX, NY, NZ = 4, 8, 8


def iota(shape, dim):
    return lax.broadcasted_iota(jnp.int32, shape, dim)


def one_hot(condition):
    return jnp.where(condition, 1.0, 0.0).astype(BF16)


def matmul(a, b):
    return jnp.dot(a, b, preferred_element_type=F32)


def contract_rows(a, b):
    return lax.dot_general(a, b, (((0,), (0,)), ((), ())), preferred_element_type=F32)


def device_at(x, y, z, core):
    return (x * 4 + lax.rem(z, 4), lax.div(z, 4) * 16 + y * 2 + core)


def remote(src, dst, sems, k, device):
    return pltpu.make_async_remote_copy(
        src_ref=src,
        dst_ref=dst,
        send_sem=sems[0].at[k],
        recv_sem=sems[1].at[k],
        device_id=device,
        device_id_type=MESH,
    )


def kernel(
    align_hbm, gain_hbm, shift_hbm, wl_hbm, bl_hbm, wr_hbm, br_hbm, ow_hbm, ob_hbm,
    out_ref,
    align, gain, shift, wl, bl, wr, br, ow, ob,
    l_first, r_first, l_z, r_z, l_by_y, r_by_x, l_y, r_all, l_t, t_ref, half_out, half_in, total,
    load_sems, zr_s, zr_r, zl_s, zl_r, xr_s, xr_r, yl_s, yl_r, yr_s, yr_r, xl_s, xl_r, core_s, core_r,
):
    seq, res = lax.axis_index("seq"), lax.axis_index("res")
    x, z_lo = lax.div(seq, 4), lax.rem(seq, 4)
    z_hi, y, core = lax.div(res, 16), lax.rem(lax.div(res, 2), 8), lax.rem(res, 2)
    z = z_hi * 4 + z_lo

    def along_x(k):
        return lax.rem(x + k, NX)

    def along_y(k):
        return lax.rem(y + k, NY)

    def along_z(k):
        return lax.rem(z + k, NZ)

    sibling = device_at(x, y, z, 1 - core)
    x_peer = {k: device_at(along_x(k), y, z, core) for k in range(1, NX)}
    y_peer = {k: device_at(x, along_y(k), z, core) for k in range(1, NY)}
    z_peer = {k: device_at(x, y, along_z(k), core) for k in range(1, NZ)}
    far_first = (4, 3, 5, 2, 6, 1, 7)

    barrier = pltpu.get_barrier_semaphore()
    everyone = [z_peer[k] for k in far_first] + [y_peer[k] for k in far_first]
    everyone += [x_peer[k] for k in (2, 1, 3)] + [sibling]
    for device in everyone:
        pl.semaphore_signal(barrier, inc=1, device_id=device, device_id_type=MESH)

    pairs = (
        (align_hbm, align), (gain_hbm, gain), (shift_hbm, shift), (wl_hbm, wl), (bl_hbm, bl),
        (wr_hbm, wr), (br_hbm, br), (ow_hbm, ow), (ob_hbm, ob),
    )
    loads = [pltpu.make_async_copy(a, b, load_sems.at[n]) for n, (a, b) in enumerate(pairs)]
    for load in loads:
        load.start()
    for load in loads:
        load.wait()

    values = align[...].astype(F32).reshape(512, 256)
    centre = jnp.mean(values, axis=-1, keepdims=True)
    spread = jnp.mean((values - centre) ** 2, axis=-1, keepdims=True)
    normed = ((values - centre) * lax.rsqrt(spread + 1e-05) * gain[...] + shift[...]).astype(BF16)
    repeat = one_hot(jnp.bitwise_and(iota((32, 128), 1), 31) == iota((32, 128), 0))
    weights = jnp.concatenate(
        [contract_rows(w[...], repeat).astype(BF16) for w in (wl, wr)], axis=1
    )
    biases = jnp.concatenate([bl[...]] * 4 + [br[...]] * 4, axis=1)
    projected = matmul(normed, weights) + biases
    lane_group = jnp.bitwise_and(jnp.right_shift(iota((512, 256), 1), 5), 3)
    mine = jnp.bitwise_and(iota((512, 256), 0), 3) == lane_group
    spaced = jnp.where(mine, projected, 0.0).astype(BF16)
    source = iota((128, 512), 1)
    target = jnp.bitwise_and(jnp.right_shift(source, 2), 63) * 2 + jnp.right_shift(source, 8)
    gathered = matmul(one_hot(target == iota((128, 512), 0)), spaced)
    l_first[...] = gathered[:, :128].astype(BF16).reshape(2, 64, 128)
    by_x = gathered[:, 128:]
    for b in range(4):
        r_first[b] = jnp.concatenate(
            [by_x[a * 32 + b * 8 : a * 32 + b * 8 + 8] for a in range(4)], axis=0
        ).astype(BF16)
    l_z[z] = l_first[z_hi]
    r_z[z] = r_first[z_lo]

    pl.semaphore_wait(barrier, len(everyone))

    zr, zl = [], []
    for k in far_first:
        to = along_z(k)
        copy = remote(r_first.at[lax.rem(to, 4)], r_z.at[z], (zr_s, zr_r), k - 1, z_peer[k])
        copy.start()
        zr.append(copy)
    for k in far_first:
        to = along_z(k)
        copy = remote(l_first.at[lax.div(to, 4)], l_z.at[z], (zl_s, zl_r), k - 1, z_peer[k])
        copy.start()
        zl.append(copy)

    o, n = iota((256, 256), 0), iota((256, 256), 1)
    o_vh, o_z, o_s = jnp.right_shift(o, 4), jnp.bitwise_and(jnp.right_shift(o, 1), 7), jnp.bitwise_and(o, 1)
    regroup = one_hot(n == o_z * 32 + o_vh * 2 + o_s)
    o, n = iota((512, 512), 0), iota((512, 512), 1)
    turn = one_hot(n == jnp.bitwise_and(o, 15) * 32 + jnp.right_shift(o, 4))

    for copy in zr:
        copy.wait_recv()
    moved = matmul(regroup, r_z[...].reshape(256, 128)).astype(BF16)
    for v in range(4):
        for h in range(4):
            r_by_x[v, :, h * 128 : (h + 1) * 128] = moved[v * 64 + h * 16 : v * 64 + h * 16 + 16]
    r_all[y, x] = r_by_x[x]
    xr = []
    for k in (2, 1, 3):
        copy = remote(r_by_x.at[along_x(k)], r_all.at[y, x], (xr_s, xr_r), k - 1, x_peer[k])
        copy.start()
        xr.append(copy)

    for copy in zl:
        copy.wait_recv()
    for part in range(2):
        moved = matmul(regroup, l_z[:, part * 32 : part * 32 + 32, :].reshape(256, 128)).astype(BF16)
        for v in range(4):
            for h in range(4):
                l_by_y[part * 4 + v, :, h * 128 : (h + 1) * 128] = moved[
                    v * 64 + h * 16 : v * 64 + h * 16 + 16
                ]
    l_y[y] = l_by_y[y]
    yl = []
    for k in far_first:
        copy = remote(l_by_y.at[along_y(k)], l_y.at[y], (yl_s, yl_r), k - 1, y_peer[k])
        copy.start()
        yl.append(copy)

    for copy in xr:
        copy.wait_recv()
    yr = []
    for k in far_first:
        copy = remote(r_all.at[y], r_all.at[y], (yr_s, yr_r), k - 1, y_peer[k])
        copy.start()
        yr.append(copy)

    for copy in yl:
        copy.wait_recv()
    l_t[x] = lax.dot_general(
        turn, l_y[...].reshape(128, 512), (((1,), (1,)), ((), ())), preferred_element_type=F32
    ).astype(BF16)
    xl = []
    for k in (2, 1, 3):
        copy = remote(l_t.at[x], l_t.at[x], (xl_s, xl_r), k - 1, x_peer[k])
        copy.start()
        xl.append(copy)

    for copy in xl + yr:
        copy.wait_recv()
    left = jnp.concatenate([l_t[a] for a in range(NX)], axis=1)
    right = jnp.concatenate([r_all[b, a] for a in range(NX) for b in range(NY)], axis=0)
    outer = (matmul(left, right) * (1.0 / 1024)).astype(BF16)
    lane = iota((128, 128), 1)
    low, even = lane < 64, jnp.bitwise_and(lane, 32) == 0
    blocks = outer.reshape(8, 4, 16, 512)
    for h in range(4):
        a, b, c, d = (
            blocks[:, n, :, h * 128 : (h + 1) * 128].reshape(128, 128).astype(F32) for n in range(4)
        )
        a, c = jnp.where(low, a, pltpu.roll(c, 64, 1)), jnp.where(low, pltpu.roll(a, 64, 1), c)
        b, d = jnp.where(low, b, pltpu.roll(d, 64, 1)), jnp.where(low, pltpu.roll(b, 64, 1), d)
        a, b = jnp.where(even, a, pltpu.roll(b, 32, 1)), jnp.where(even, pltpu.roll(a, 96, 1), b)
        c, d = jnp.where(even, c, pltpu.roll(d, 32, 1)), jnp.where(even, pltpu.roll(c, 96, 1), d)
        for n, block in enumerate((a, b, c, d)):
            block = block.astype(BF16)
            row = (h * 4 + n) * 16
            for m in range(8):
                t_ref[row : row + 16, m * 128 : (m + 1) * 128] = block[m * 16 : m * 16 + 16]
    term = matmul(t_ref[...], ow[...]).reshape(16, 2, 8, 128)
    half_out[...] = jnp.where(core == 0, term[:, 1], term[:, 0]).reshape(128, 128)
    swap = remote(half_out, half_in, (core_s, core_r), 0, sibling)
    swap.start()
    kept = jnp.where(core == 0, term[:, 0], term[:, 1]).reshape(128, 128)
    swap.wait_recv()
    total[...] = kept + half_in[...]
    for i in range(8):
        out_ref[i] = (total[pl.ds(i, 16, stride=8), :] + ob[...]).astype(BF16)
    for copy in zr + zl + xr + yl + yr + xl + [swap]:
        copy.wait_send()


def body(alignment, gain, shift, wl, bl, wr, br, ow, ob):
    any_space = pl.BlockSpec(memory_space=pl.ANY)
    dma = pltpu.SemaphoreType.DMA
    args = (
        alignment, gain.reshape(1, -1), shift.reshape(1, -1), wl.T, bl.reshape(1, -1),
        wr.T, br.reshape(1, -1), ow, ob.reshape(1, -1),
    )
    scratch = [pltpu.VMEM(a.shape, a.dtype) for a in args]
    scratch += [
        pltpu.VMEM((2, 64, 128), BF16),
        pltpu.VMEM((4, 32, 128), BF16),
        pltpu.VMEM((8, 64, 128), BF16),
        pltpu.VMEM((8, 32, 128), BF16),
        pltpu.VMEM((8, 16, 512), BF16),
        pltpu.VMEM((4, 16, 512), BF16),
        pltpu.VMEM((8, 16, 512), BF16),
        pltpu.VMEM((8, 4, 16, 512), BF16),
        pltpu.VMEM((4, 512, 128), BF16),
        pltpu.VMEM((256, 1024), BF16),
        pltpu.VMEM((128, 128), F32),
        pltpu.VMEM((128, 128), F32),
        pltpu.VMEM((128, 128), F32),
        dma((len(args),)),
    ]
    for n in (7, 7, 3, 7, 7, 3, 1):
        scratch += [dma((n,)), dma((n,))]
    return pl.pallas_call(
        kernel,
        out_shape=jax.ShapeDtypeStruct((8, 16, 128), BF16),
        in_specs=[any_space] * len(args),
        out_specs=pl.BlockSpec(memory_space=pltpu.VMEM),
        scratch_shapes=scratch,
        compiler_params=pltpu.CompilerParams(
            collective_id=0, has_side_effects=True, vmem_limit_bytes=62 << 20
        ),
    )(*args)


def solution(mesh):
    in_specs = (P(("seq", "res"), None, None), P(), P(), P(), P(), P(), P(), P(), P())
    return jax.shard_map(
        body, mesh=mesh, in_specs=in_specs, out_specs=P("res", "seq", None), check_vma=False
    )
```

```python
import functools

import jax
import jax.numpy as jnp
from jax import lax
from jax.experimental import pallas as pl
from jax.experimental.pallas import tpu as pltpu
from jax.sharding import PartitionSpec as P

MESH = pl.DeviceIdType.MESH
F32 = jnp.float32
BF16 = jnp.bfloat16
NX, NY, NZ = 4, 8, 8


def iota(shape, dim):
    return lax.broadcasted_iota(jnp.int32, shape, dim)


def one_hot(condition):
    return jnp.where(condition, 1.0, 0.0).astype(BF16)


def matmul(a, b):
    return jnp.dot(a, b, preferred_element_type=F32)


def contract_rows(a, b):
    return lax.dot_general(a, b, (((0,), (0,)), ((), ())), preferred_element_type=F32)


def device_at(x, y, z, core):
    return (x * 4 + lax.rem(z, 4), lax.div(z, 4) * 16 + y * 2 + core)


def remote(src, dst, sems, k, device):
    return pltpu.make_async_remote_copy(
        src_ref=src,
        dst_ref=dst,
        send_sem=sems[0].at[k],
        recv_sem=sems[1].at[k],
        device_id=device,
        device_id_type=MESH,
    )


def kernel(
    align_hbm, gain_hbm, shift_hbm, wl_hbm, bl_hbm, wr_hbm, br_hbm, ow_hbm, ob_hbm,
    out_ref,
    align, gain, shift, wl, bl, wr, br, ow, ob,
    l_first, r_first, l_y, r_z, l_by_z, r_by_x, l_z, r_all, l_t, t_ref, half_out, half_in, total,
    load_sems, zr_s, zr_r, zl_s, zl_r, xr_s, xr_r, yl_s, yl_r, yr_s, yr_r, xl_s, xl_r, core_s, core_r,
):
    seq, res = lax.axis_index("seq"), lax.axis_index("res")
    x, z_lo = lax.div(seq, 4), lax.rem(seq, 4)
    z_hi, y, core = lax.div(res, 16), lax.rem(lax.div(res, 2), 8), lax.rem(res, 2)
    z = z_hi * 4 + z_lo

    def along_x(k):
        return lax.rem(x + k, NX)

    def along_y(k):
        return lax.rem(y + k, NY)

    def along_z(k):
        return lax.rem(z + k, NZ)

    sibling = device_at(x, y, z, 1 - core)
    x_peer = {k: device_at(along_x(k), y, z, core) for k in range(1, NX)}
    y_peer = {k: device_at(x, along_y(k), z, core) for k in range(1, NY)}
    z_peer = {k: device_at(x, y, along_z(k), core) for k in range(1, NZ)}
    far_first = (4, 3, 5, 2, 6, 1, 7)

    barrier = pltpu.get_barrier_semaphore()
    everyone = [z_peer[k] for k in far_first] + [y_peer[k] for k in far_first]
    everyone += [x_peer[k] for k in (2, 1, 3)] + [sibling]
    for device in everyone:
        pl.semaphore_signal(barrier, inc=1, device_id=device, device_id_type=MESH)

    pairs = (
        (align_hbm, align), (gain_hbm, gain), (shift_hbm, shift), (wl_hbm, wl), (bl_hbm, bl),
        (wr_hbm, wr), (br_hbm, br), (ow_hbm, ow), (ob_hbm, ob),
    )
    loads = [pltpu.make_async_copy(a, b, load_sems.at[n]) for n, (a, b) in enumerate(pairs)]
    for load in loads:
        load.start()
    for load in loads:
        load.wait()

    values = align[...].astype(F32).reshape(512, 256)
    centre = jnp.mean(values, axis=-1, keepdims=True)
    spread = jnp.mean((values - centre) ** 2, axis=-1, keepdims=True)
    normed = ((values - centre) * lax.rsqrt(spread + 1e-05) * gain[...] + shift[...]).astype(BF16)
    repeat = one_hot(jnp.bitwise_and(iota((32, 128), 1), 31) == iota((32, 128), 0))
    weights = jnp.concatenate(
        [contract_rows(w[...], repeat).astype(BF16) for w in (wl, wr)], axis=1
    )
    biases = jnp.concatenate([bl[...]] * 4 + [br[...]] * 4, axis=1)
    projected = matmul(normed, weights) + biases
    lane_group = jnp.bitwise_and(jnp.right_shift(iota((512, 256), 1), 5), 3)
    mine = jnp.bitwise_and(iota((512, 256), 0), 3) == lane_group
    spaced = jnp.where(mine, projected, 0.0).astype(BF16)
    source = iota((128, 512), 1)
    target = jnp.bitwise_and(jnp.right_shift(source, 2), 63) * 2 + jnp.right_shift(source, 8)
    gathered = matmul(one_hot(target == iota((128, 512), 0)), spaced)
    for b in range(NY):
        l_first[b] = jnp.concatenate(
            [gathered[a * 64 + b * 8 : a * 64 + b * 8 + 8, :128] for a in range(2)], axis=0
        ).astype(BF16)
    by_x = gathered[:, 128:]
    for b in range(4):
        r_first[b] = jnp.concatenate(
            [by_x[a * 32 + b * 8 : a * 32 + b * 8 + 8] for a in range(4)], axis=0
        ).astype(BF16)
    l_y[y] = l_first[y]
    r_z[z] = r_first[z_lo]

    pl.semaphore_wait(barrier, len(everyone))

    zr, yl = [], []
    for k in far_first:
        to = along_z(k)
        copy = remote(r_first.at[lax.rem(to, 4)], r_z.at[z], (zr_s, zr_r), k - 1, z_peer[k])
        copy.start()
        zr.append(copy)
    for k in far_first:
        copy = remote(l_first.at[along_y(k)], l_y.at[y], (yl_s, yl_r), k - 1, y_peer[k])
        copy.start()
        yl.append(copy)

    o, n = iota((256, 256), 0), iota((256, 256), 1)
    o_vh, o_z, o_s = jnp.right_shift(o, 4), jnp.bitwise_and(jnp.right_shift(o, 1), 7), jnp.bitwise_and(o, 1)
    regroup = one_hot(n == o_z * 32 + o_vh * 2 + o_s)
    o, n = iota((128, 128), 0), iota((128, 128), 1)
    o_zh, o_y, o_s = jnp.right_shift(o, 4), jnp.bitwise_and(jnp.right_shift(o, 1), 7), jnp.bitwise_and(o, 1)
    regroup_l = one_hot(n == o_y * 16 + o_zh * 2 + o_s)
    o, n = iota((512, 512), 0), iota((512, 512), 1)
    turn = one_hot(n == jnp.bitwise_and(o, 15) * 32 + jnp.right_shift(o, 4))

    for copy in zr:
        copy.wait_recv()
    moved = matmul(regroup, r_z[...].reshape(256, 128)).astype(BF16)
    for v in range(4):
        for h in range(4):
            r_by_x[v, :, h * 128 : (h + 1) * 128] = moved[v * 64 + h * 16 : v * 64 + h * 16 + 16]
    r_all[y, x] = r_by_x[x]
    xr = []
    for k in (2, 1, 3):
        copy = remote(r_by_x.at[along_x(k)], r_all.at[y, x], (xr_s, xr_r), k - 1, x_peer[k])
        copy.start()
        xr.append(copy)

    for copy in yl:
        copy.wait_recv()
    moved = matmul(regroup_l, l_y[...].reshape(128, 128)).astype(BF16)
    for v in range(2):
        for h in range(4):
            l_by_z[v, :, h * 128 : (h + 1) * 128] = moved[v * 64 + h * 16 : v * 64 + h * 16 + 16]
    l_z[z] = l_by_z[z_hi]
    zl = []
    for k in far_first:
        to = along_z(k)
        copy = remote(l_by_z.at[lax.div(to, 4)], l_z.at[z], (zl_s, zl_r), k - 1, z_peer[k])
        copy.start()
        zl.append(copy)

    for copy in xr:
        copy.wait_recv()
    yr = []
    for k in far_first:
        copy = remote(r_all.at[y], r_all.at[y], (yr_s, yr_r), k - 1, y_peer[k])
        copy.start()
        yr.append(copy)

    for copy in zl:
        copy.wait_recv()
    ordered = matmul(regroup_l, l_z[...].reshape(128, 512)).astype(BF16)
    l_t[x] = lax.dot_general(
        turn, ordered, (((1,), (1,)), ((), ())), preferred_element_type=F32
    ).astype(BF16)
    xl = []
    for k in (2, 1, 3):
        copy = remote(l_t.at[x], l_t.at[x], (xl_s, xl_r), k - 1, x_peer[k])
        copy.start()
        xl.append(copy)

    for copy in xl + yr:
        copy.wait_recv()
    left = jnp.concatenate([l_t[a] for a in range(NX)], axis=1)
    right = jnp.concatenate([r_all[b, a] for a in range(NX) for b in range(NY)], axis=0)
    outer = (matmul(left, right) * (1.0 / 1024)).astype(BF16)
    lane = iota((128, 128), 1)
    low, even = lane < 64, jnp.bitwise_and(lane, 32) == 0
    blocks = outer.reshape(8, 4, 16, 512)
    for h in range(4):
        a, b, c, d = (
            blocks[:, n, :, h * 128 : (h + 1) * 128].reshape(128, 128).astype(F32) for n in range(4)
        )
        a, c = jnp.where(low, a, pltpu.roll(c, 64, 1)), jnp.where(low, pltpu.roll(a, 64, 1), c)
        b, d = jnp.where(low, b, pltpu.roll(d, 64, 1)), jnp.where(low, pltpu.roll(b, 64, 1), d)
        a, b = jnp.where(even, a, pltpu.roll(b, 32, 1)), jnp.where(even, pltpu.roll(a, 96, 1), b)
        c, d = jnp.where(even, c, pltpu.roll(d, 32, 1)), jnp.where(even, pltpu.roll(c, 96, 1), d)
        for n, block in enumerate((a, b, c, d)):
            block = block.astype(BF16)
            row = (h * 4 + n) * 16
            for m in range(8):
                t_ref[row : row + 16, m * 128 : (m + 1) * 128] = block[m * 16 : m * 16 + 16]
    term = matmul(t_ref[...], ow[...]).reshape(16, 2, 8, 128)
    half_out[...] = jnp.where(core == 0, term[:, 1], term[:, 0]).reshape(128, 128)
    swap = remote(half_out, half_in, (core_s, core_r), 0, sibling)
    swap.start()
    kept = jnp.where(core == 0, term[:, 0], term[:, 1]).reshape(128, 128)
    swap.wait_recv()
    total[...] = kept + half_in[...]
    for i in range(8):
        out_ref[i] = (total[pl.ds(i, 16, stride=8), :] + ob[...]).astype(BF16)
    for copy in zr + zl + xr + yl + yr + xl + [swap]:
        copy.wait_send()


def body(alignment, gain, shift, wl, bl, wr, br, ow, ob):
    any_space = pl.BlockSpec(memory_space=pl.ANY)
    dma = pltpu.SemaphoreType.DMA
    args = (
        alignment, gain.reshape(1, -1), shift.reshape(1, -1), wl.T, bl.reshape(1, -1),
        wr.T, br.reshape(1, -1), ow, ob.reshape(1, -1),
    )
    scratch = [pltpu.VMEM(a.shape, a.dtype) for a in args]
    scratch += [
        pltpu.VMEM((8, 16, 128), BF16),
        pltpu.VMEM((4, 32, 128), BF16),
        pltpu.VMEM((8, 16, 128), BF16),
        pltpu.VMEM((8, 32, 128), BF16),
        pltpu.VMEM((2, 16, 512), BF16),
        pltpu.VMEM((4, 16, 512), BF16),
        pltpu.VMEM((8, 16, 512), BF16),
        pltpu.VMEM((8, 4, 16, 512), BF16),
        pltpu.VMEM((4, 512, 128), BF16),
        pltpu.VMEM((256, 1024), BF16),
        pltpu.VMEM((128, 128), F32),
        pltpu.VMEM((128, 128), F32),
        pltpu.VMEM((128, 128), F32),
        dma((len(args),)),
    ]
    for n in (7, 7, 3, 7, 7, 3, 1):
        scratch += [dma((n,)), dma((n,))]
    args = tuple(pltpu.with_memory_space_constraint(a, pltpu.HBM) for a in args)
    return pl.pallas_call(
        kernel,
        out_shape=jax.ShapeDtypeStruct((8, 16, 128), BF16),
        in_specs=[any_space] * len(args),
        out_specs=pl.BlockSpec(memory_space=pltpu.VMEM),
        scratch_shapes=scratch,
        compiler_params=pltpu.CompilerParams(
            collective_id=0, has_side_effects=True, vmem_limit_bytes=32 << 20
        ),
    )(*args)


def solution(mesh):
    in_specs = (P(("seq", "res"), None, None), P(), P(), P(), P(), P(), P(), P(), P())
    return jax.shard_map(
        body, mesh=mesh, in_specs=in_specs, out_specs=P("res", "seq", None), check_vma=False
    )
```

```python
import functools

import jax
import jax.numpy as jnp
from jax import lax
from jax.experimental import pallas as pl
from jax.experimental.pallas import tpu as pltpu
from jax.sharding import PartitionSpec as P

MESH = pl.DeviceIdType.MESH
F32 = jnp.float32
BF16 = jnp.bfloat16
NX, NY, NZ = 4, 8, 8


def iota(shape, dim):
    return lax.broadcasted_iota(jnp.int32, shape, dim)


def one_hot(condition):
    return jnp.where(condition, 1.0, 0.0).astype(BF16)


def matmul(a, b):
    return jnp.dot(a, b, preferred_element_type=F32)


def contract_rows(a, b):
    return lax.dot_general(a, b, (((0,), (0,)), ((), ())), preferred_element_type=F32)


def device_at(x, y, z, core):
    return (x * 4 + lax.rem(z, 4), lax.div(z, 4) * 16 + y * 2 + core)


def remote(src, dst, sems, k, device):
    return pltpu.make_async_remote_copy(
        src_ref=src,
        dst_ref=dst,
        send_sem=sems[0].at[k],
        recv_sem=sems[1].at[k],
        device_id=device,
        device_id_type=MESH,
    )


def kernel(
    align_hbm, gain_hbm, shift_hbm, wl_hbm, bl_hbm, wr_hbm, br_hbm, ow_hbm, ob_hbm,
    out_ref,
    align, gain, shift, wl, bl, wr, br, ow, ob,
    l_first, ra_first, rb_first, l_y, ra_z, rb_y, l_by_z, ra_by_x, rb_by_x, l_z, ra_all, rb_x, rb_all, l_t, t_ref, half_out, half_in, total,
    load_sems, za_s, za_r, zl_s, zl_r, xa_s, xa_r, yl_s, yl_r, ya_s, ya_r, xl_s, xl_r, yb_s, yb_r, xb_s, xb_r,
    zb_s, zb_r, core_s, core_r,
):
    seq, res = lax.axis_index("seq"), lax.axis_index("res")
    x, z_lo = lax.div(seq, 4), lax.rem(seq, 4)
    z_hi, y, core = lax.div(res, 16), lax.rem(lax.div(res, 2), 8), lax.rem(res, 2)
    z = z_hi * 4 + z_lo

    def along_x(k):
        return lax.rem(x + k, NX)

    def along_y(k):
        return lax.rem(y + k, NY)

    def along_z(k):
        return lax.rem(z + k, NZ)

    sibling = device_at(x, y, z, 1 - core)
    x_peer = {k: device_at(along_x(k), y, z, core) for k in range(1, NX)}
    y_peer = {k: device_at(x, along_y(k), z, core) for k in range(1, NY)}
    z_peer = {k: device_at(x, y, along_z(k), core) for k in range(1, NZ)}
    far_first = (4, 3, 5, 2, 6, 1, 7)

    barrier = pltpu.get_barrier_semaphore()
    everyone = [z_peer[k] for k in far_first] + [y_peer[k] for k in far_first]
    everyone += [x_peer[k] for k in (2, 1, 3)] + [sibling]
    for device in everyone:
        pl.semaphore_signal(barrier, inc=1, device_id=device, device_id_type=MESH)

    pairs = (
        (align_hbm, align), (gain_hbm, gain), (shift_hbm, shift), (wl_hbm, wl), (bl_hbm, bl),
        (wr_hbm, wr), (br_hbm, br), (ow_hbm, ow), (ob_hbm, ob),
    )
    loads = [pltpu.make_async_copy(a, b, load_sems.at[n]) for n, (a, b) in enumerate(pairs)]
    for load in loads:
        load.start()
    for load in loads:
        load.wait()

    values = align[...].astype(F32).reshape(512, 256)
    centre = jnp.mean(values, axis=-1, keepdims=True)
    spread = jnp.mean((values - centre) ** 2, axis=-1, keepdims=True)
    normed = ((values - centre) * lax.rsqrt(spread + 1e-05) * gain[...] + shift[...]).astype(BF16)
    repeat = one_hot(jnp.bitwise_and(iota((32, 128), 1), 31) == iota((32, 128), 0))
    weights = jnp.concatenate(
        [contract_rows(w[...], repeat).astype(BF16) for w in (wl, wr)], axis=1
    )
    biases = jnp.concatenate([bl[...]] * 4 + [br[...]] * 4, axis=1)
    projected = matmul(normed, weights) + biases
    lane_group = jnp.bitwise_and(jnp.right_shift(iota((512, 256), 1), 5), 3)
    mine = jnp.bitwise_and(iota((512, 256), 0), 3) == lane_group
    spaced = jnp.where(mine, projected, 0.0).astype(BF16)
    o, n = iota((128, 512), 0), iota((128, 512), 1)
    n_s, n_h = jnp.right_shift(n, 8), jnp.bitwise_and(jnp.right_shift(n, 2), 3)
    n_y, n_zh = jnp.bitwise_and(jnp.right_shift(n, 4), 7), jnp.bitwise_and(jnp.right_shift(n, 7), 1)
    pick_l = one_hot(o == n_y * 16 + n_zh * 8 + n_h * 2 + n_s)
    n_zl, n_x = jnp.bitwise_and(jnp.right_shift(n, 4), 3), jnp.bitwise_and(jnp.right_shift(n, 6), 3)
    row_a = n_zl * 16 + n_x * 4 + n_h * 2 + n_s
    row_b = 64 + n_x * 16 + n_zl * 4 + (n_h - 2) * 2 + n_s
    pick_r = one_hot(o == jnp.where(n_h < 2, row_a, row_b))
    l_first[...] = matmul(pick_l, spaced[:, :128]).astype(BF16).reshape(8, 16, 128)
    picked = matmul(pick_r, spaced[:, 128:]).astype(BF16)
    ra_first[...] = picked[:64].reshape(4, 16, 128)
    rb_first[...] = picked[64:]
    l_y[y] = l_first[y]
    ra_z[z] = ra_first[z_lo]
    rb_y[y] = rb_first[...]

    pl.semaphore_wait(barrier, len(everyone))

    def to_all(peers, order, sems, src, dst):
        copies = []
        for k in order:
            copy = remote(src(k), dst, sems, k - 1, peers[k])
            copy.start()
            copies.append(copy)
        return copies

    def arrive(copies):
        for copy in copies:
            copy.wait_recv()

    x_order = (2, 1, 3)
    za = to_all(z_peer, far_first, (za_s, za_r), lambda k: ra_first.at[lax.rem(along_z(k), 4)], ra_z.at[z])
    yl = to_all(y_peer, far_first, (yl_s, yl_r), lambda k: l_first.at[along_y(k)], l_y.at[y])
    yb = to_all(y_peer, far_first, (yb_s, yb_r), lambda k: rb_first, rb_y.at[y])

    o, n = iota((128, 128), 0), iota((128, 128), 1)
    o_v, o_m, o_s = jnp.right_shift(o, 4), jnp.bitwise_and(jnp.right_shift(o, 1), 7), jnp.bitwise_and(o, 1)
    regroup = one_hot(n == o_m * 16 + o_v * 2 + o_s)
    o, n = iota((512, 512), 0), iota((512, 512), 1)
    turn = one_hot(n == jnp.bitwise_and(o, 15) * 32 + jnp.right_shift(o, 4))

    arrive(za)
    moved = matmul(regroup, ra_z[...].reshape(128, 128)).astype(BF16)
    for v in range(4):
        for h in range(2):
            ra_by_x[v, :, h * 128 : (h + 1) * 128] = moved[v * 32 + h * 16 : v * 32 + h * 16 + 16]
    ra_all[y, x] = ra_by_x[x]
    xa = to_all(x_peer, x_order, (xa_s, xa_r), lambda k: ra_by_x.at[along_x(k)], ra_all.at[y, x])

    arrive(yl)
    moved = matmul(regroup, l_y[...].reshape(128, 128)).astype(BF16)
    for v in range(2):
        for h in range(4):
            l_by_z[v, :, h * 128 : (h + 1) * 128] = moved[v * 64 + h * 16 : v * 64 + h * 16 + 16]
    l_z[z] = l_by_z[z_hi]
    zl = to_all(z_peer, far_first, (zl_s, zl_r), lambda k: l_by_z.at[lax.div(along_z(k), 4)], l_z.at[z])

    arrive(yb)
    wide = jnp.concatenate(
        [rb_y[:, a * 16 : a * 16 + 16, :].reshape(128, 128) for a in range(NX)], axis=1
    )
    moved = matmul(regroup, wide).astype(BF16)
    for a in range(NX):
        for v in range(4):
            for h in range(2):
                rb_by_x[a, v, :, h * 128 : (h + 1) * 128] = moved[
                    v * 32 + h * 16 : v * 32 + h * 16 + 16, a * 128 : (a + 1) * 128
                ]
    rb_x[:, x] = rb_by_x[x]
    xb = to_all(x_peer, x_order, (xb_s, xb_r), lambda k: rb_by_x.at[along_x(k)], rb_x.at[:, x])

    arrive(xa)
    ya = to_all(y_peer, far_first, (ya_s, ya_r), lambda k: ra_all.at[y], ra_all.at[y])

    arrive(xb)
    rb_all[z] = rb_x[z_lo]
    zb = to_all(z_peer, far_first, (zb_s, zb_r), lambda k: rb_x.at[lax.rem(along_z(k), 4)], rb_all.at[z])

    arrive(zl)
    l_t[x] = lax.dot_general(
        turn, l_z[...].reshape(128, 512), (((1,), (1,)), ((), ())), preferred_element_type=F32
    ).astype(BF16)
    xl = to_all(x_peer, x_order, (xl_s, xl_r), lambda k: l_t.at[x], l_t.at[x])

    arrive(ya)
    right_a = [
        matmul(regroup, jnp.concatenate([ra_all[b, a] for b in range(NY)], axis=0)).astype(BF16)
        for a in range(NX)
    ]
    arrive(zb)
    right_b = [rb_all[b, a] for a in range(NX) for b in range(NZ)]
    right = jnp.concatenate(
        [jnp.concatenate(right_a, axis=0), jnp.concatenate(right_b, axis=0)], axis=1
    )
    arrive(xl)
    left = jnp.concatenate([l_t[a] for a in range(NX)], axis=1)
    outer = (matmul(left, right) * (1.0 / 1024)).astype(BF16)
    lane = iota((128, 128), 1)
    low, even = lane < 64, jnp.bitwise_and(lane, 32) == 0
    blocks = outer.reshape(8, 4, 16, 512)
    for h in range(4):
        a, b, c, d = (
            blocks[:, n, :, h * 128 : (h + 1) * 128].reshape(128, 128).astype(F32) for n in range(4)
        )
        a, c = jnp.where(low, a, pltpu.roll(c, 64, 1)), jnp.where(low, pltpu.roll(a, 64, 1), c)
        b, d = jnp.where(low, b, pltpu.roll(d, 64, 1)), jnp.where(low, pltpu.roll(b, 64, 1), d)
        a, b = jnp.where(even, a, pltpu.roll(b, 32, 1)), jnp.where(even, pltpu.roll(a, 96, 1), b)
        c, d = jnp.where(even, c, pltpu.roll(d, 32, 1)), jnp.where(even, pltpu.roll(c, 96, 1), d)
        for n, block in enumerate((a, b, c, d)):
            block = block.astype(BF16)
            row = (h * 4 + n) * 16
            for m in range(8):
                t_ref[row : row + 16, m * 128 : (m + 1) * 128] = block[m * 16 : m * 16 + 16]
    term = matmul(t_ref[...], ow[...]).reshape(16, 2, 8, 128)
    half_out[...] = jnp.where(core == 0, term[:, 1], term[:, 0]).reshape(128, 128)
    swap = remote(half_out, half_in, (core_s, core_r), 0, sibling)
    swap.start()
    kept = jnp.where(core == 0, term[:, 0], term[:, 1]).reshape(128, 128)
    arrive([swap])
    total[...] = kept + half_in[...]
    for i in range(8):
        out_ref[i] = (total[pl.ds(i, 16, stride=8), :] + ob[...]).astype(BF16)
    for copy in za + yl + yb + xa + zl + xb + ya + zb + xl + [swap]:
        copy.wait_send()


def body(alignment, gain, shift, wl, bl, wr, br, ow, ob):
    any_space = pl.BlockSpec(memory_space=pl.ANY)
    dma = pltpu.SemaphoreType.DMA
    args = (
        alignment, gain.reshape(1, -1), shift.reshape(1, -1), wl.T, bl.reshape(1, -1),
        wr.T, br.reshape(1, -1), ow, ob.reshape(1, -1),
    )
    scratch = [pltpu.VMEM(a.shape, a.dtype) for a in args]
    scratch += [
        pltpu.VMEM((8, 16, 128), BF16),
        pltpu.VMEM((4, 16, 128), BF16),
        pltpu.VMEM((64, 128), BF16),
        pltpu.VMEM((8, 16, 128), BF16),
        pltpu.VMEM((8, 16, 128), BF16),
        pltpu.VMEM((8, 64, 128), BF16),
        pltpu.VMEM((2, 16, 512), BF16),
        pltpu.VMEM((4, 16, 256), BF16),
        pltpu.VMEM((4, 4, 16, 256), BF16),
        pltpu.VMEM((8, 16, 512), BF16),
        pltpu.VMEM((8, 4, 16, 256), BF16),
        pltpu.VMEM((4, 4, 16, 256), BF16),
        pltpu.VMEM((8, 4, 16, 256), BF16),
        pltpu.VMEM((4, 512, 128), BF16),
        pltpu.VMEM((256, 1024), BF16),
        pltpu.VMEM((128, 128), F32),
        pltpu.VMEM((128, 128), F32),
        pltpu.VMEM((128, 128), F32),
        dma((len(args),)),
    ]
    for n in (7, 7, 3, 7, 7, 3, 7, 3, 7, 1):
        scratch += [dma((n,)), dma((n,))]
    args = tuple(pltpu.with_memory_space_constraint(a, pltpu.HBM) for a in args)
    return pl.pallas_call(
        kernel,
        out_shape=jax.ShapeDtypeStruct((8, 16, 128), BF16),
        in_specs=[any_space] * len(args),
        out_specs=pl.BlockSpec(memory_space=pltpu.VMEM),
        scratch_shapes=scratch,
        compiler_params=pltpu.CompilerParams(
            collective_id=0, has_side_effects=True, vmem_limit_bytes=32 << 20
        ),
    )(*args)


def solution(mesh):
    in_specs = (P(("seq", "res"), None, None), P(), P(), P(), P(), P(), P(), P(), P())
    return jax.shard_map(
        body, mesh=mesh, in_specs=in_specs, out_specs=P("res", "seq", None), check_vma=False
    )
```

```python
import functools

import jax
import jax.numpy as jnp
from jax import lax
from jax.experimental import pallas as pl
from jax.experimental.pallas import tpu as pltpu
from jax.sharding import PartitionSpec as P

MESH = pl.DeviceIdType.MESH
F32 = jnp.float32
BF16 = jnp.bfloat16
NX, NY, NZ = 4, 8, 8


def iota(shape, dim):
    return lax.broadcasted_iota(jnp.int32, shape, dim)


def one_hot(condition):
    return jnp.where(condition, 1.0, 0.0).astype(BF16)


def matmul(a, b):
    return jnp.dot(a, b, preferred_element_type=F32)


def contract_rows(a, b):
    return lax.dot_general(a, b, (((0,), (0,)), ((), ())), preferred_element_type=F32)


def device_at(x, y, z, core):
    return (x * 4 + lax.rem(z, 4), lax.div(z, 4) * 16 + y * 2 + core)


def remote(src, dst, sems, k, device):
    return pltpu.make_async_remote_copy(
        src_ref=src,
        dst_ref=dst,
        send_sem=sems[0].at[k],
        recv_sem=sems[1].at[k],
        device_id=device,
        device_id_type=MESH,
    )


def kernel(
    align_hbm, gain_hbm, shift_hbm, wl_hbm, bl_hbm, wr_hbm, br_hbm, ow_hbm, ob_hbm,
    out_ref,
    align, gain, shift, wl, bl, wr, br, ow, ob,
    l_first, ra_first, rb_first, l_y, ra_z, rb_y, l_by_z, ra_by_x, rb_by_x, l_all, ra_all, rb_x, rb_all, t_ref, half_out, half_in, total,
    load_sems, za_s, za_r, near_s, near_r, far_s, far_r, xa_s, xa_r, yl_s, yl_r, ya_s, ya_r, xn_s, xn_r, xf_s, xf_r, yb_s, yb_r, xb_s, xb_r,
    zb_s, zb_r, core_s, core_r,
):
    seq, res = lax.axis_index("seq"), lax.axis_index("res")
    x, z_lo = lax.div(seq, 4), lax.rem(seq, 4)
    z_hi, y, core = lax.div(res, 16), lax.rem(lax.div(res, 2), 8), lax.rem(res, 2)
    z = z_hi * 4 + z_lo

    z_slots = (0, 1, 3, 5, 7, 6, 4, 2)

    def along_x(k):
        return lax.rem(x + k, NX)

    def along_y(k):
        return lax.rem(y + k, NY)

    def along_z(k):
        return lax.rem(z + k, NZ)

    sibling = device_at(x, y, z, 1 - core)
    x_peer = {k: device_at(along_x(k), y, z, core) for k in range(1, NX)}
    y_peer = {k: device_at(x, along_y(k), z, core) for k in range(1, NY)}
    z_peer = {k: device_at(x, y, along_z(k), core) for k in range(1, NZ)}
    far_first = (4, 3, 5, 2, 6, 1, 7)

    pairs = (
        (align_hbm, align), (gain_hbm, gain), (shift_hbm, shift), (wl_hbm, wl), (bl_hbm, bl),
        (wr_hbm, wr), (br_hbm, br), (ow_hbm, ow), (ob_hbm, ob),
    )
    loads = [pltpu.make_async_copy(a, b, load_sems.at[n]) for n, (a, b) in enumerate(pairs)]
    for load in loads:
        load.start()

    barrier = pltpu.get_barrier_semaphore()
    everyone = [z_peer[k] for k in far_first] + [y_peer[k] for k in far_first]
    everyone += [x_peer[k] for k in (2, 1, 3)] + [sibling]
    for device in everyone:
        pl.semaphore_signal(barrier, inc=1, device_id=device, device_id_type=MESH)

    for load in loads[:7]:
        load.wait()
    values = align[...].astype(F32).reshape(512, 256)
    centre = jnp.mean(values, axis=-1, keepdims=True)
    spread = jnp.mean((values - centre) ** 2, axis=-1, keepdims=True)
    normed = ((values - centre) * lax.rsqrt(spread + 1e-05) * gain[...] + shift[...]).astype(BF16)
    repeat = one_hot(jnp.bitwise_and(iota((32, 128), 1), 31) == iota((32, 128), 0))
    weights = jnp.concatenate(
        [contract_rows(w[...], repeat).astype(BF16) for w in (wl, wr)], axis=1
    )
    biases = jnp.concatenate([bl[...]] * 4 + [br[...]] * 4, axis=1)
    projected = matmul(normed, weights) + biases
    lane_group = jnp.bitwise_and(jnp.right_shift(iota((512, 256), 1), 5), 3)
    mine = jnp.bitwise_and(iota((512, 256), 0), 3) == lane_group
    spaced = jnp.where(mine, projected, 0.0).astype(BF16)
    o, n = iota((128, 512), 0), iota((128, 512), 1)
    n_s, n_h = jnp.right_shift(n, 8), jnp.bitwise_and(jnp.right_shift(n, 2), 3)
    n_y, n_zh = jnp.bitwise_and(jnp.right_shift(n, 4), 7), jnp.bitwise_and(jnp.right_shift(n, 7), 1)
    pick_l = one_hot(o == n_y * 16 + n_zh * 8 + n_h * 2 + n_s)
    n_zl, n_x = jnp.bitwise_and(jnp.right_shift(n, 4), 3), jnp.bitwise_and(jnp.right_shift(n, 6), 3)
    row_a = n_zl * 16 + n_x * 4 + n_h * 2 + n_s
    row_b = 64 + n_x * 16 + n_zl * 4 + (n_h - 2) * 2 + n_s
    pick_r = one_hot(o == jnp.where(n_h < 2, row_a, row_b))
    l_first[...] = matmul(pick_l, spaced[:, :128]).astype(BF16).reshape(8, 16, 128)
    picked = matmul(pick_r, spaced[:, 128:]).astype(BF16)
    ra_first[...] = picked[:64].reshape(4, 16, 128)
    rb_first[...] = picked[64:]
    l_y[y] = l_first[y]
    ra_z[z] = ra_first[z_lo]
    rb_y[y] = rb_first[...]

    pl.semaphore_wait(barrier, len(everyone))

    def to_all(axis, sems, src, dst):
        copies = []
        me, count, order, peer = axis
        for n in range(count - 1):
            place = order(n)
            k = lax.rem(place - me + count, count)
            copy = remote(
                src(place), dst(place) if callable(dst) else dst, sems, k - 1, peer(place)
            )
            copy.start()
            copies.append(copy)
        return copies

    def rising(me):
        return lambda n: n + jnp.where(n >= me, 1, 0)

    on_z = z, NZ, rising(z), lambda place: device_at(x, y, place, core)
    on_y = y, NY, rising(y), lambda place: device_at(x, place, z, core)
    on_x = x, NX, lambda n: lax.rem(x + (2, 1, 3)[n], NX), lambda place: device_at(place, y, z, core)

    def arrive(copies):
        for copy in copies:
            copy.wait_recv()

    yl = to_all(on_y, (yl_s, yl_r), lambda to: l_first.at[to], l_y.at[y])
    za = to_all(on_z, (za_s, za_r), lambda to: ra_first.at[lax.rem(to, 4)], ra_z.at[z])
    yb = to_all(on_y, (yb_s, yb_r), lambda to: rb_first, rb_y.at[y])

    def slot(dz):
        return jnp.where(dz == 0, 0, jnp.where(dz <= 4, 2 * dz - 1, 2 * (8 - dz)))

    o, n = iota((128, 128), 0), iota((128, 128), 1)
    o_v, o_m, o_s = jnp.right_shift(o, 4), jnp.bitwise_and(jnp.right_shift(o, 1), 7), jnp.bitwise_and(o, 1)
    regroup = one_hot(n == o_m * 16 + o_v * 2 + o_s)
    o, n = iota((512, 512), 0), iota((512, 512), 1)
    turn = one_hot(n == jnp.bitwise_and(o, 15) * 32 + jnp.right_shift(o, 4))

    arrive(yl)
    moved = matmul(regroup, l_y[...].reshape(128, 128)).astype(BF16)
    for v in range(2):
        for h in range(4):
            l_by_z[v, :, h * 128 : (h + 1) * 128] = moved[v * 64 + h * 16 : v * 64 + h * 16 + 16]
    l_all[x, 0] = l_by_z[z_hi]

    def to_z(steps, sems):
        copies = []
        for n, k in enumerate(steps):
            src = l_by_z.at[lax.div(along_z(k), 4)]
            copies.append(remote(src, l_all.at[x, z_slots[8 - k]], sems, n, z_peer[k]))
            copies[-1].start()
        return copies

    near = to_z((2, 6, 1, 7), (near_s, near_r))
    far = to_z((4, 3, 5), (far_s, far_r))

    arrive(za)
    moved = matmul(regroup, ra_z[...].reshape(128, 128)).astype(BF16)
    for v in range(4):
        for h in range(2):
            ra_by_x[v, :, h * 128 : (h + 1) * 128] = moved[v * 32 + h * 16 : v * 32 + h * 16 + 16]
    ra_all[y, x] = ra_by_x[x]
    xa = to_all(on_x, (xa_s, xa_r), lambda to: ra_by_x.at[to], ra_all.at[y, x])

    arrive(yb)
    wide = jnp.concatenate(
        [rb_y[:, a * 16 : a * 16 + 16, :].reshape(128, 128) for a in range(NX)], axis=1
    )
    moved = matmul(regroup, wide).astype(BF16)
    for a in range(NX):
        for v in range(4):
            for h in range(2):
                rb_by_x[a, v, :, h * 128 : (h + 1) * 128] = moved[
                    v * 32 + h * 16 : v * 32 + h * 16 + 16, a * 128 : (a + 1) * 128
                ]
    rb_x[:, x] = rb_by_x[x]
    xb = to_all(on_x, (xb_s, xb_r), lambda to: rb_by_x.at[to], rb_x.at[:, x])

    arrive(xa)
    ya = to_all(on_y, (ya_s, ya_r), lambda to: ra_all.at[y], ra_all.at[y])

    arrive(xb)
    rb_all[0] = rb_x[z_lo]
    zb = to_all(
        on_z, (zb_s, zb_r), lambda to: rb_x.at[lax.rem(to, 4)],
        lambda to: rb_all.at[slot(lax.rem(z - to + NZ, NZ))],
    )

    arrive(near)
    xn = to_all(on_x, (xn_s, xn_r), lambda to: l_all.at[x, pl.ds(0, 5)], l_all.at[x, pl.ds(0, 5)])

    arrive(far)
    xf = to_all(on_x, (xf_s, xf_r), lambda to: l_all.at[x, pl.ds(5, 3)], l_all.at[x, pl.ds(5, 3)])

    o, n = iota((128, 128), 0), iota((128, 128), 1)
    o_slot = jnp.right_shift(o, 4)
    o_half = jnp.right_shift(o_slot + 1, 1)
    o_z = jnp.bitwise_and(z + jnp.where(jnp.bitwise_and(o_slot, 1) == 1, o_half, 8 - o_half), 7)
    o_y = jnp.bitwise_and(jnp.right_shift(o, 1), 7)
    by_slot = one_hot(n == o_y * 16 + o_z * 2 + jnp.bitwise_and(o, 1))
    arrive(ya)
    right_a = [
        matmul(by_slot, jnp.concatenate([ra_all[b, a] for b in range(NY)], axis=0)).astype(BF16)
        for a in range(NX)
    ]
    arrive(zb)
    right_b = [rb_all[b, a] for a in range(NX) for b in range(NZ)]
    right = jnp.concatenate(
        [jnp.concatenate(right_a, axis=0), jnp.concatenate(right_b, axis=0)], axis=1
    )
    arrive(xn + xf)
    left = lax.dot_general(
        turn, l_all[...].reshape(512, 512), (((1,), (1,)), ((), ())), preferred_element_type=F32
    ).astype(BF16)
    outer = (matmul(left, right) * (1.0 / 1024)).astype(BF16)
    lane = iota((128, 128), 1)
    low, even = lane < 64, jnp.bitwise_and(lane, 32) == 0
    blocks = outer.reshape(8, 4, 16, 512)
    for h in range(4):
        a, b, c, d = (
            blocks[:, n, :, h * 128 : (h + 1) * 128].reshape(128, 128) for n in range(4)
        )
        a, c = jnp.where(low, a, pltpu.roll(c, 64, 1)), jnp.where(low, pltpu.roll(a, 64, 1), c)
        b, d = jnp.where(low, b, pltpu.roll(d, 64, 1)), jnp.where(low, pltpu.roll(b, 64, 1), d)
        a, b = jnp.where(even, a, pltpu.roll(b, 32, 1)), jnp.where(even, pltpu.roll(a, 96, 1), b)
        c, d = jnp.where(even, c, pltpu.roll(d, 32, 1)), jnp.where(even, pltpu.roll(c, 96, 1), d)
        for n, block in enumerate((a, b, c, d)):
            row = (h * 4 + n) * 16
            for m in range(8):
                t_ref[row : row + 16, m * 128 : (m + 1) * 128] = block[m * 16 : m * 16 + 16]
    for load in loads[7:]:
        load.wait()
    term = matmul(t_ref[...], ow[...]).reshape(16, 2, 8, 128)
    half_out[...] = jnp.where(core == 0, term[:, 1], term[:, 0]).reshape(128, 128)
    swap = remote(half_out, half_in, (core_s, core_r), 0, sibling)
    swap.start()
    kept = jnp.where(core == 0, term[:, 0], term[:, 1]).reshape(128, 128)
    arrive([swap])
    total[...] = kept + half_in[...]
    for i in range(8):
        out_ref[i] = (total[pl.ds(i, 16, stride=8), :] + ob[...]).astype(BF16)
    for copy in za + yl + yb + xa + near + far + xn + xf + xb + ya + zb + [swap]:
        copy.wait_send()


def body(alignment, gain, shift, wl, bl, wr, br, ow, ob):
    any_space = pl.BlockSpec(memory_space=pl.ANY)
    dma = pltpu.SemaphoreType.DMA
    args = (
        alignment, gain.reshape(1, -1), shift.reshape(1, -1), wl.T, bl.reshape(1, -1),
        wr.T, br.reshape(1, -1), ow, ob.reshape(1, -1),
    )
    scratch = [pltpu.VMEM(a.shape, a.dtype) for a in args]
    scratch += [
        pltpu.VMEM((8, 16, 128), BF16),
        pltpu.VMEM((4, 16, 128), BF16),
        pltpu.VMEM((64, 128), BF16),
        pltpu.VMEM((8, 16, 128), BF16),
        pltpu.VMEM((8, 16, 128), BF16),
        pltpu.VMEM((8, 64, 128), BF16),
        pltpu.VMEM((2, 16, 512), BF16),
        pltpu.VMEM((4, 16, 256), BF16),
        pltpu.VMEM((4, 4, 16, 256), BF16),
        pltpu.VMEM((4, 8, 16, 512), BF16),
        pltpu.VMEM((8, 4, 16, 256), BF16),
        pltpu.VMEM((4, 4, 16, 256), BF16),
        pltpu.VMEM((8, 4, 16, 256), BF16),
        pltpu.VMEM((256, 1024), BF16),
        pltpu.VMEM((128, 128), F32),
        pltpu.VMEM((128, 128), F32),
        pltpu.VMEM((128, 128), F32),
        dma((len(args),)),
    ]
    for n in (7, 4, 3, 3, 7, 7, 3, 3, 7, 3, 7, 1):
        scratch += [dma((n,)), dma((n,))]
    args = tuple(pltpu.with_memory_space_constraint(a, pltpu.HBM) for a in args)
    return pl.pallas_call(
        kernel,
        out_shape=jax.ShapeDtypeStruct((8, 16, 128), BF16),
        in_specs=[any_space] * len(args),
        out_specs=pl.BlockSpec(memory_space=pltpu.VMEM),
        scratch_shapes=scratch,
        compiler_params=pltpu.CompilerParams(
            collective_id=0, has_side_effects=True, vmem_limit_bytes=32 << 20
        ),
    )(*args)


def solution(mesh):
    in_specs = (P(("seq", "res"), None, None), P(), P(), P(), P(), P(), P(), P(), P())
    return jax.shard_map(
        body, mesh=mesh, in_specs=in_specs, out_specs=P("res", "seq", None), check_vma=False
    )
```

```python
import functools

import jax
import jax.numpy as jnp
from jax import lax
from jax.experimental import pallas as pl
from jax.experimental.pallas import tpu as pltpu
from jax.sharding import PartitionSpec as P

MESH = pl.DeviceIdType.MESH
F32 = jnp.float32
BF16 = jnp.bfloat16
NX, NY, NZ = 4, 8, 8


def low_bits(n, size):
    return jnp.bitwise_and(n, size - 1)


def high_bits(n, size):
    return jnp.right_shift(n, size.bit_length() - 1)


def iota(shape, dim):
    return lax.broadcasted_iota(jnp.int32, shape, dim)


def one_hot(condition):
    return jnp.where(condition, 1.0, 0.0).astype(BF16)


def matmul(a, b):
    return jnp.dot(a, b, preferred_element_type=F32)


def contract_rows(a, b):
    return lax.dot_general(a, b, (((0,), (0,)), ((), ())), preferred_element_type=F32)


def device_at(x, y, z, core):
    return (x * 4 + low_bits(z, 4), high_bits(z, 4) * 16 + y * 2 + core)


def remote(src, dst, sems, k, device):
    return pltpu.make_async_remote_copy(
        src_ref=src,
        dst_ref=dst,
        send_sem=sems[0].at[k],
        recv_sem=sems[1].at[k],
        device_id=device,
        device_id_type=MESH,
    )


def kernel(
    align_hbm, gain_hbm, shift_hbm, wl_hbm, bl_hbm, wr_hbm, br_hbm, ow_hbm, ob_hbm,
    out_ref,
    align, gain, shift, wl, bl, wr, br, ow, ob,
    l_first, ra_first, rb_first, l_y, ra_z, rb_y, l_by_z, ra_by_x, rb_by_x, l_all, ra_all, rb_x, rb_all, t_ref, half_out, half_in, total,
    load_sems, za_s, za_r, near_s, near_r, far_s, far_r, xa_s, xa_r, yl_s, yl_r, ya_s, ya_r, xn_s, xn_r, xf_s, xf_r, yb_s, yb_r, xb_s, xb_r,
    zb_s, zb_r, core_s, core_r,
):
    seq, res = lax.axis_index("seq"), lax.axis_index("res")
    x, z_lo = high_bits(seq, 4), low_bits(seq, 4)
    z_hi, y, core = high_bits(res, 16), low_bits(high_bits(res, 2), 8), low_bits(res, 2)
    z = z_hi * 4 + z_lo

    z_slots = (0, 1, 3, 5, 7, 6, 4, 2)

    def along_x(k):
        return low_bits(x + k, NX)

    def along_y(k):
        return low_bits(y + k, NY)

    def along_z(k):
        return low_bits(z + k, NZ)

    sibling = device_at(x, y, z, 1 - core)
    x_peer = {k: device_at(along_x(k), y, z, core) for k in range(1, NX)}
    y_peer = {k: device_at(x, along_y(k), z, core) for k in range(1, NY)}
    z_peer = {k: device_at(x, y, along_z(k), core) for k in range(1, NZ)}
    far_first = (4, 3, 5, 2, 6, 1, 7)

    pairs = (
        (align_hbm, align), (gain_hbm, gain), (shift_hbm, shift), (wl_hbm, wl), (bl_hbm, bl),
        (wr_hbm, wr), (br_hbm, br), (ow_hbm, ow), (ob_hbm, ob),
    )
    loads = [pltpu.make_async_copy(a, b, load_sems.at[n]) for n, (a, b) in enumerate(pairs)]
    for load in loads:
        load.start()

    barrier = pltpu.get_barrier_semaphore()
    everyone = [z_peer[k] for k in far_first] + [y_peer[k] for k in far_first]
    everyone += [x_peer[k] for k in (2, 1, 3)] + [sibling]
    for device in everyone:
        pl.semaphore_signal(barrier, inc=1, device_id=device, device_id_type=MESH)

    o, n = iota((128, 512), 0), iota((128, 512), 1)
    n_s, n_h = jnp.right_shift(n, 8), jnp.bitwise_and(jnp.right_shift(n, 2), 3)
    n_y, n_zh = jnp.bitwise_and(jnp.right_shift(n, 4), 7), jnp.bitwise_and(jnp.right_shift(n, 7), 1)
    pick_l = one_hot(o == n_y * 16 + n_zh * 8 + n_h * 2 + n_s)
    n_zl, n_x = jnp.bitwise_and(jnp.right_shift(n, 4), 3), jnp.bitwise_and(jnp.right_shift(n, 6), 3)
    row_a = n_zl * 16 + n_x * 4 + n_h * 2 + n_s
    row_b = 64 + n_x * 16 + n_zl * 4 + (n_h - 2) * 2 + n_s
    pick_r = one_hot(o == jnp.where(n_h < 2, row_a, row_b))
    repeat = one_hot(jnp.bitwise_and(iota((32, 128), 1), 31) == iota((32, 128), 0))
    for load in loads[1:7]:
        load.wait()
    weights = jnp.concatenate(
        [contract_rows(w[...], repeat).astype(BF16) for w in (wl, wr)], axis=1
    )
    biases = jnp.concatenate([bl[...]] * 4 + [br[...]] * 4, axis=1)
    loads[0].wait()
    values = align[...].astype(F32).reshape(512, 256)
    centre = jnp.mean(values, axis=-1, keepdims=True)
    spread = jnp.mean((values - centre) ** 2, axis=-1, keepdims=True)
    normed = ((values - centre) * lax.rsqrt(spread + 1e-05) * gain[...] + shift[...]).astype(BF16)
    projected = matmul(normed, weights) + biases
    lane_group = jnp.bitwise_and(jnp.right_shift(iota((512, 256), 1), 5), 3)
    mine = jnp.bitwise_and(iota((512, 256), 0), 3) == lane_group
    spaced = jnp.where(mine, projected, 0.0).astype(BF16)
    l_first[...] = matmul(pick_l, spaced[:, :128]).astype(BF16).reshape(8, 16, 128)
    picked = matmul(pick_r, spaced[:, 128:]).astype(BF16)
    ra_first[...] = picked[:64].reshape(4, 16, 128)
    rb_first[...] = picked[64:]
    l_y[y] = l_first[y]
    ra_z[z] = ra_first[z_lo]
    rb_y[y] = rb_first[...]

    pl.semaphore_wait(barrier, len(everyone))

    def to_all(axis, sems, src, dst):
        copies = []
        me, count, order, peer = axis
        for n in range(count - 1):
            place = order(n)
            k = low_bits(place - me + count, count)
            copy = remote(
                src(place), dst(place) if callable(dst) else dst, sems, k - 1, peer(place)
            )
            copy.start()
            copies.append(copy)
        return copies

    def rising(me):
        return lambda n: n + jnp.where(n >= me, 1, 0)

    on_z = z, NZ, rising(z), lambda place: device_at(x, y, place, core)
    on_y = y, NY, rising(y), lambda place: device_at(x, place, z, core)
    on_x = x, NX, lambda n: low_bits(x + (2, 1, 3)[n], NX), lambda place: device_at(place, y, z, core)

    def arrive(copies):
        for copy in copies:
            copy.wait_recv()

    yl = to_all(on_y, (yl_s, yl_r), lambda to: l_first.at[to], l_y.at[y])
    za = to_all(on_z, (za_s, za_r), lambda to: ra_first.at[low_bits(to, 4)], ra_z.at[z])
    yb = to_all(on_y, (yb_s, yb_r), lambda to: rb_first, rb_y.at[y])

    def slot(dz):
        return jnp.where(dz == 0, 0, jnp.where(dz <= 4, 2 * dz - 1, 2 * (8 - dz)))

    o, n = iota((128, 128), 0), iota((128, 128), 1)
    o_v, o_m, o_s = jnp.right_shift(o, 4), jnp.bitwise_and(jnp.right_shift(o, 1), 7), jnp.bitwise_and(o, 1)
    regroup = one_hot(n == o_m * 16 + o_v * 2 + o_s)
    o, n = iota((512, 512), 0), iota((512, 512), 1)
    turn = one_hot(n == jnp.bitwise_and(o, 15) * 32 + jnp.right_shift(o, 4))

    arrive(yl)
    moved = matmul(regroup, l_y[...].reshape(128, 128)).astype(BF16)
    for v in range(2):
        for h in range(4):
            l_by_z[v, :, h * 128 : (h + 1) * 128] = moved[v * 64 + h * 16 : v * 64 + h * 16 + 16]
    l_all[x, 0] = l_by_z[z_hi]

    def to_z(steps, sems):
        copies = []
        for n, k in enumerate(steps):
            src = l_by_z.at[high_bits(along_z(k), 4)]
            copies.append(remote(src, l_all.at[x, z_slots[8 - k]], sems, n, z_peer[k]))
            copies[-1].start()
        return copies

    near = to_z((2, 6, 1, 7), (near_s, near_r))
    far = to_z((4, 3, 5), (far_s, far_r))

    arrive(za)
    moved = matmul(regroup, ra_z[...].reshape(128, 128)).astype(BF16)
    for v in range(4):
        for h in range(2):
            ra_by_x[v, :, h * 128 : (h + 1) * 128] = moved[v * 32 + h * 16 : v * 32 + h * 16 + 16]
    ra_all[y, x] = ra_by_x[x]
    xa = to_all(on_x, (xa_s, xa_r), lambda to: ra_by_x.at[to], ra_all.at[y, x])

    arrive(yb)
    wide = jnp.concatenate(
        [rb_y[:, a * 16 : a * 16 + 16, :].reshape(128, 128) for a in range(NX)], axis=1
    )
    moved = matmul(regroup, wide).astype(BF16)
    for a in range(NX):
        for v in range(4):
            for h in range(2):
                rb_by_x[a, v, :, h * 128 : (h + 1) * 128] = moved[
                    v * 32 + h * 16 : v * 32 + h * 16 + 16, a * 128 : (a + 1) * 128
                ]
    rb_x[:, x] = rb_by_x[x]
    xb = to_all(on_x, (xb_s, xb_r), lambda to: rb_by_x.at[to], rb_x.at[:, x])

    arrive(xa)
    ya = to_all(on_y, (ya_s, ya_r), lambda to: ra_all.at[y], ra_all.at[y])

    arrive(xb)
    rb_all[0] = rb_x[z_lo]
    zb = to_all(
        on_z, (zb_s, zb_r), lambda to: rb_x.at[low_bits(to, 4)],
        lambda to: rb_all.at[slot(low_bits(z - to + NZ, NZ))],
    )

    arrive(near)
    xn = to_all(on_x, (xn_s, xn_r), lambda to: l_all.at[x, pl.ds(0, 5)], l_all.at[x, pl.ds(0, 5)])

    arrive(far)
    xf = to_all(on_x, (xf_s, xf_r), lambda to: l_all.at[x, pl.ds(5, 3)], l_all.at[x, pl.ds(5, 3)])

    o, n = iota((128, 128), 0), iota((128, 128), 1)
    o_slot = jnp.right_shift(o, 4)
    o_half = jnp.right_shift(o_slot + 1, 1)
    o_z = jnp.bitwise_and(z + jnp.where(jnp.bitwise_and(o_slot, 1) == 1, o_half, 8 - o_half), 7)
    o_y = jnp.bitwise_and(jnp.right_shift(o, 1), 7)
    by_slot = one_hot(n == o_y * 16 + o_z * 2 + jnp.bitwise_and(o, 1))
    arrive(ya)
    right_a = [
        matmul(by_slot, jnp.concatenate([ra_all[b, a] for b in range(NY)], axis=0)).astype(BF16)
        for a in range(NX)
    ]
    arrive(zb)
    right_b = [rb_all[b, a] for a in range(NX) for b in range(NZ)]
    right = jnp.concatenate(
        [jnp.concatenate(right_a, axis=0), jnp.concatenate(right_b, axis=0)], axis=1
    )
    arrive(xn + xf)
    left = lax.dot_general(
        turn, l_all[...].reshape(512, 512), (((1,), (1,)), ((), ())), preferred_element_type=F32
    ).astype(BF16)
    outer = (matmul(left, right) * (1.0 / 1024)).astype(BF16)
    lane = iota((128, 128), 1)
    low, even = lane < 64, jnp.bitwise_and(lane, 32) == 0
    blocks = outer.reshape(8, 4, 16, 512)
    for h in range(4):
        a, b, c, d = (
            blocks[:, n, :, h * 128 : (h + 1) * 128].reshape(128, 128) for n in range(4)
        )
        a, c = jnp.where(low, a, pltpu.roll(c, 64, 1)), jnp.where(low, pltpu.roll(a, 64, 1), c)
        b, d = jnp.where(low, b, pltpu.roll(d, 64, 1)), jnp.where(low, pltpu.roll(b, 64, 1), d)
        a, b = jnp.where(even, a, pltpu.roll(b, 32, 1)), jnp.where(even, pltpu.roll(a, 96, 1), b)
        c, d = jnp.where(even, c, pltpu.roll(d, 32, 1)), jnp.where(even, pltpu.roll(c, 96, 1), d)
        for n, block in enumerate((a, b, c, d)):
            row = (h * 4 + n) * 16
            for m in range(8):
                t_ref[row : row + 16, m * 128 : (m + 1) * 128] = block[m * 16 : m * 16 + 16]
    for load in loads[7:]:
        load.wait()
    term = matmul(t_ref[...], ow[...]).reshape(16, 2, 8, 128)
    half_out[...] = jnp.where(core == 0, term[:, 1], term[:, 0]).reshape(128, 128)
    swap = remote(half_out, half_in, (core_s, core_r), 0, sibling)
    swap.start()
    kept = jnp.where(core == 0, term[:, 0], term[:, 1]).reshape(128, 128)
    for copy in za + yl + yb + xa + near + far + xn + xf + xb + ya + zb:
        copy.wait_send()
    arrive([swap])
    total[...] = kept + half_in[...]
    for i in range(8):
        out_ref[i] = (total[pl.ds(i, 16, stride=8), :] + ob[...]).astype(BF16)
    swap.wait_send()


def body(alignment, gain, shift, wl, bl, wr, br, ow, ob):
    any_space = pl.BlockSpec(memory_space=pl.ANY)
    dma = pltpu.SemaphoreType.DMA
    args = (
        alignment, gain.reshape(1, -1), shift.reshape(1, -1), wl.T, bl.reshape(1, -1),
        wr.T, br.reshape(1, -1), ow, ob.reshape(1, -1),
    )
    scratch = [pltpu.VMEM(a.shape, a.dtype) for a in args]
    scratch += [
        pltpu.VMEM((8, 16, 128), BF16),
        pltpu.VMEM((4, 16, 128), BF16),
        pltpu.VMEM((64, 128), BF16),
        pltpu.VMEM((8, 16, 128), BF16),
        pltpu.VMEM((8, 16, 128), BF16),
        pltpu.VMEM((8, 64, 128), BF16),
        pltpu.VMEM((2, 16, 512), BF16),
        pltpu.VMEM((4, 16, 256), BF16),
        pltpu.VMEM((4, 4, 16, 256), BF16),
        pltpu.VMEM((4, 8, 16, 512), BF16),
        pltpu.VMEM((8, 4, 16, 256), BF16),
        pltpu.VMEM((4, 4, 16, 256), BF16),
        pltpu.VMEM((8, 4, 16, 256), BF16),
        pltpu.VMEM((256, 1024), BF16),
        pltpu.VMEM((128, 128), F32),
        pltpu.VMEM((128, 128), F32),
        pltpu.VMEM((128, 128), F32),
        dma((len(args),)),
    ]
    for n in (7, 4, 3, 3, 7, 7, 3, 3, 7, 3, 7, 1):
        scratch += [dma((n,)), dma((n,))]
    args = tuple(pltpu.with_memory_space_constraint(a, pltpu.HBM) for a in args)
    return pl.pallas_call(
        kernel,
        out_shape=jax.ShapeDtypeStruct((8, 16, 128), BF16),
        in_specs=[any_space] * len(args),
        out_specs=pl.BlockSpec(memory_space=pltpu.VMEM),
        scratch_shapes=scratch,
        compiler_params=pltpu.CompilerParams(
            collective_id=0, has_side_effects=True, vmem_limit_bytes=32 << 20
        ),
    )(*args)


def solution(mesh):
    in_specs = (P(("seq", "res"), None, None), P(), P(), P(), P(), P(), P(), P(), P())
    return jax.shard_map(
        body, mesh=mesh, in_specs=in_specs, out_specs=P("res", "seq", None), check_vma=False
    )
```

```python
import functools

import jax
import jax.numpy as jnp
from jax import lax
from jax.experimental import pallas as pl
from jax.experimental.pallas import tpu as pltpu
from jax.sharding import PartitionSpec as P

MESH = pl.DeviceIdType.MESH
F32 = jnp.float32
BF16 = jnp.bfloat16
NX, NY, NZ = 4, 8, 8


def low_bits(n, size):
    return jnp.bitwise_and(n, size - 1)


def high_bits(n, size):
    return jnp.right_shift(n, size.bit_length() - 1)


def iota(shape, dim):
    return lax.broadcasted_iota(jnp.int32, shape, dim)


def one_hot(condition):
    return jnp.where(condition, 1.0, 0.0).astype(BF16)


def matmul(a, b):
    return jnp.dot(a, b, preferred_element_type=F32)


def contract_rows(a, b):
    return lax.dot_general(a, b, (((0,), (0,)), ((), ())), preferred_element_type=F32)


def device_at(x, y, z, core):
    return (x * 4 + low_bits(z, 4), high_bits(z, 4) * 16 + y * 2 + core)


def remote(src, dst, sems, k, device):
    return pltpu.make_async_remote_copy(
        src_ref=src,
        dst_ref=dst,
        send_sem=sems[0].at[k],
        recv_sem=sems[1].at[k],
        device_id=device,
        device_id_type=MESH,
    )


def kernel(
    align_hbm, gain_hbm, shift_hbm, wl_hbm, bl_hbm, wr_hbm, br_hbm, ow_hbm, ob_hbm,
    out_ref,
    align, gain, shift, wl, bl, wr, br, ow, ob,
    l_first, ra_first, rb_first, l_y, ra_z, rb_y, l_by_z, ra_by_x, rb_by_x, l_all, ra_all, rb_x, rb_all, t_ref, half_out, half_in, total,
    load_sems, za_s, za_r, near_s, near_r, far_s, far_r, xa_s, xa_r, yl_s, yl_r, ya_s, ya_r, xn_s, xn_r, xf_s, xf_r, yb_s, yb_r, xb_s, xb_r,
    zb_s, zb_r, core_s, core_r,
):
    seq, res = lax.axis_index("seq"), lax.axis_index("res")
    x, z_lo = high_bits(seq, 4), low_bits(seq, 4)
    z_hi, y, core = high_bits(res, 16), low_bits(high_bits(res, 2), 8), low_bits(res, 2)
    z = z_hi * 4 + z_lo

    z_slots = (0, 1, 3, 5, 7, 6, 4, 2)

    def along_x(k):
        return low_bits(x + k, NX)

    def along_y(k):
        return low_bits(y + k, NY)

    def along_z(k):
        return low_bits(z + k, NZ)

    sibling = device_at(x, y, z, 1 - core)
    x_peer = {k: device_at(along_x(k), y, z, core) for k in range(1, NX)}
    y_peer = {k: device_at(x, along_y(k), z, core) for k in range(1, NY)}
    z_peer = {k: device_at(x, y, along_z(k), core) for k in range(1, NZ)}
    far_first = (4, 3, 5, 2, 6, 1, 7)

    pairs = (
        (align_hbm, align), (gain_hbm, gain), (shift_hbm, shift), (wl_hbm, wl), (bl_hbm, bl),
        (wr_hbm, wr), (br_hbm, br), (ow_hbm, ow), (ob_hbm, ob),
    )
    loads = [pltpu.make_async_copy(a, b, load_sems.at[n]) for n, (a, b) in enumerate(pairs)]
    for load in loads:
        load.start()

    barrier = pltpu.get_barrier_semaphore()
    everyone = [z_peer[k] for k in far_first] + [y_peer[k] for k in far_first]
    everyone += [x_peer[k] for k in (2, 1, 3)] + [sibling]
    for device in everyone:
        pl.semaphore_signal(barrier, inc=1, device_id=device, device_id_type=MESH)

    o, n = iota((128, 512), 0), iota((128, 512), 1)
    n_s, n_h = jnp.right_shift(n, 8), jnp.bitwise_and(jnp.right_shift(n, 2), 3)
    n_y, n_zh = jnp.bitwise_and(jnp.right_shift(n, 4), 7), jnp.bitwise_and(jnp.right_shift(n, 7), 1)
    pick_l = one_hot(o == n_y * 16 + n_zh * 8 + n_h * 2 + n_s)
    n_zl, n_x = jnp.bitwise_and(jnp.right_shift(n, 4), 3), jnp.bitwise_and(jnp.right_shift(n, 6), 3)
    row_a = n_zl * 16 + n_x * 4 + n_h * 2 + n_s
    row_b = 64 + n_x * 16 + n_zl * 4 + (n_h - 2) * 2 + n_s
    pick_r = one_hot(o == jnp.where(n_h < 2, row_a, row_b))
    repeat = one_hot(jnp.bitwise_and(iota((32, 128), 1), 31) == iota((32, 128), 0))
    for load in loads[1:7]:
        load.wait()
    weights = jnp.concatenate(
        [contract_rows(w[...], repeat).astype(BF16) for w in (wl, wr)], axis=1
    )
    biases = jnp.concatenate([bl[...]] * 4 + [br[...]] * 4, axis=1)
    loads[0].wait()
    values = align[...].astype(F32).reshape(512, 256)
    centre = jnp.mean(values, axis=-1, keepdims=True)
    spread = jnp.mean((values - centre) ** 2, axis=-1, keepdims=True)
    normed = ((values - centre) * lax.rsqrt(spread + 1e-05) * gain[...] + shift[...]).astype(BF16)
    projected = matmul(normed, weights) + biases
    lane_group = jnp.bitwise_and(jnp.right_shift(iota((512, 256), 1), 5), 3)
    mine = jnp.bitwise_and(iota((512, 256), 0), 3) == lane_group
    spaced = jnp.where(mine, projected, 0.0).astype(BF16)
    l_first[...] = matmul(pick_l, spaced[:, :128]).astype(BF16).reshape(8, 16, 128)
    picked = matmul(pick_r, spaced[:, 128:]).astype(BF16)
    ra_first[...] = picked[:64].reshape(4, 16, 128)
    rb_first[...] = picked[64:]
    l_y[y] = l_first[y]
    ra_z[z] = ra_first[z_lo]
    rb_y[y] = rb_first[...]

    pl.semaphore_wait(barrier, len(everyone))

    def to_all(axis, sems, src, dst):
        copies = []
        me, count, order, peer = axis
        for n in range(count - 1):
            place = order(n)
            k = low_bits(place - me + count, count)
            copy = remote(
                src(place), dst(place) if callable(dst) else dst, sems, k - 1, peer(place)
            )
            copy.start()
            copies.append(copy)
        return copies

    def rising(me):
        return lambda n: n + jnp.where(n >= me, 1, 0)

    on_z = z, NZ, rising(z), lambda place: device_at(x, y, place, core)
    on_y = y, NY, rising(y), lambda place: device_at(x, place, z, core)
    on_x = x, NX, lambda n: low_bits(x + (2, 1, 3)[n], NX), lambda place: device_at(place, y, z, core)

    def arrive(copies):
        for copy in copies:
            copy.wait_recv()

    yl = to_all(on_y, (yl_s, yl_r), lambda to: l_first.at[to], l_y.at[y])
    za = to_all(on_z, (za_s, za_r), lambda to: ra_first.at[low_bits(to, 4)], ra_z.at[z])
    yb = to_all(on_y, (yb_s, yb_r), lambda to: rb_first, rb_y.at[y])

    def slot(dz):
        return jnp.where(dz == 0, 0, jnp.where(dz <= 4, 2 * dz - 1, 2 * (8 - dz)))

    o, n = iota((128, 128), 0), iota((128, 128), 1)
    o_v, o_m, o_s = jnp.right_shift(o, 4), jnp.bitwise_and(jnp.right_shift(o, 1), 7), jnp.bitwise_and(o, 1)
    regroup = one_hot(n == o_m * 16 + o_v * 2 + o_s)
    o, n = iota((512, 512), 0), iota((512, 512), 1)
    turn = one_hot(n == jnp.bitwise_and(o, 15) * 32 + jnp.right_shift(o, 4))

    arrive(yl)
    moved = matmul(regroup, l_y[...].reshape(128, 128)).astype(BF16)
    for v in range(2):
        for h in range(4):
            l_by_z[v, :, h * 128 : (h + 1) * 128] = moved[v * 64 + h * 16 : v * 64 + h * 16 + 16]
    l_all[x, 0] = l_by_z[z_hi]

    def to_z(steps, sems):
        copies = []
        for n, k in enumerate(steps):
            src = l_by_z.at[high_bits(along_z(k), 4)]
            copies.append(remote(src, l_all.at[x, z_slots[8 - k]], sems, n, z_peer[k]))
            copies[-1].start()
        return copies

    far = to_z((4, 3, 5), (far_s, far_r))
    near = to_z((2, 6, 1, 7), (near_s, near_r))

    arrive(za)
    moved = matmul(regroup, ra_z[...].reshape(128, 128)).astype(BF16)
    for v in range(4):
        for h in range(2):
            ra_by_x[v, :, h * 128 : (h + 1) * 128] = moved[v * 32 + h * 16 : v * 32 + h * 16 + 16]
    ra_all[y, x] = ra_by_x[x]
    xa = to_all(on_x, (xa_s, xa_r), lambda to: ra_by_x.at[to], ra_all.at[y, x])

    arrive(yb)
    wide = jnp.concatenate(
        [rb_y[:, a * 16 : a * 16 + 16, :].reshape(128, 128) for a in range(NX)], axis=1
    )
    moved = matmul(regroup, wide).astype(BF16)
    for a in range(NX):
        for v in range(4):
            for h in range(2):
                rb_by_x[a, v, :, h * 128 : (h + 1) * 128] = moved[
                    v * 32 + h * 16 : v * 32 + h * 16 + 16, a * 128 : (a + 1) * 128
                ]
    rb_x[:, x] = rb_by_x[x]
    xb = to_all(on_x, (xb_s, xb_r), lambda to: rb_by_x.at[to], rb_x.at[:, x])

    arrive(xa)
    ya = to_all(on_y, (ya_s, ya_r), lambda to: ra_all.at[y], ra_all.at[y])

    arrive(xb)
    rb_all[0] = rb_x[z_lo]
    zb = to_all(
        on_z, (zb_s, zb_r), lambda to: rb_x.at[low_bits(to, 4)],
        lambda to: rb_all.at[slot(low_bits(z - to + NZ, NZ))],
    )

    arrive(near)
    xn = to_all(on_x, (xn_s, xn_r), lambda to: l_all.at[x, pl.ds(0, 5)], l_all.at[x, pl.ds(0, 5)])

    arrive(far)
    xf = to_all(on_x, (xf_s, xf_r), lambda to: l_all.at[x, pl.ds(5, 3)], l_all.at[x, pl.ds(5, 3)])

    o, n = iota((128, 128), 0), iota((128, 128), 1)
    o_slot = jnp.right_shift(o, 4)
    o_half = jnp.right_shift(o_slot + 1, 1)
    o_z = jnp.bitwise_and(z + jnp.where(jnp.bitwise_and(o_slot, 1) == 1, o_half, 8 - o_half), 7)
    o_y = jnp.bitwise_and(jnp.right_shift(o, 1), 7)
    by_slot = one_hot(n == o_y * 16 + o_z * 2 + jnp.bitwise_and(o, 1))
    arrive(ya)
    right_a = [
        matmul(by_slot, jnp.concatenate([ra_all[b, a] for b in range(NY)], axis=0)).astype(BF16)
        for a in range(NX)
    ]
    arrive(zb)
    right_b = [rb_all[b, a] for a in range(NX) for b in range(NZ)]
    right = jnp.concatenate(
        [jnp.concatenate(right_a, axis=0), jnp.concatenate(right_b, axis=0)], axis=1
    )
    arrive(xn + xf)
    left = lax.dot_general(
        turn, l_all[...].reshape(512, 512), (((1,), (1,)), ((), ())), preferred_element_type=F32
    ).astype(BF16)
    outer = (matmul(left, right) * (1.0 / 1024)).astype(BF16)
    lane = iota((128, 128), 1)
    low, even = lane < 64, jnp.bitwise_and(lane, 32) == 0
    blocks = outer.reshape(8, 4, 16, 512)
    for h in range(4):
        a, b, c, d = (
            blocks[:, n, :, h * 128 : (h + 1) * 128].reshape(128, 128) for n in range(4)
        )
        a, c = jnp.where(low, a, pltpu.roll(c, 64, 1)), jnp.where(low, pltpu.roll(a, 64, 1), c)
        b, d = jnp.where(low, b, pltpu.roll(d, 64, 1)), jnp.where(low, pltpu.roll(b, 64, 1), d)
        a, b = jnp.where(even, a, pltpu.roll(b, 32, 1)), jnp.where(even, pltpu.roll(a, 96, 1), b)
        c, d = jnp.where(even, c, pltpu.roll(d, 32, 1)), jnp.where(even, pltpu.roll(c, 96, 1), d)
        for n, block in enumerate((a, b, c, d)):
            row = (h * 4 + n) * 16
            for m in range(8):
                t_ref[row : row + 16, m * 128 : (m + 1) * 128] = block[m * 16 : m * 16 + 16]
    for load in loads[7:]:
        load.wait()
    term = matmul(t_ref[...], ow[...]).reshape(16, 2, 8, 128)
    half_out[...] = jnp.where(core == 0, term[:, 1], term[:, 0]).reshape(128, 128)
    swap = remote(half_out, half_in, (core_s, core_r), 0, sibling)
    swap.start()
    kept = jnp.where(core == 0, term[:, 0], term[:, 1]).reshape(128, 128)
    for copy in za + yl + yb + xa + near + far + xn + xf + xb + ya + zb:
        copy.wait_send()
    arrive([swap])
    total[...] = kept + half_in[...]
    for i in range(8):
        out_ref[i] = (total[pl.ds(i, 16, stride=8), :] + ob[...]).astype(BF16)
    swap.wait_send()


def body(alignment, gain, shift, wl, bl, wr, br, ow, ob):
    any_space = pl.BlockSpec(memory_space=pl.ANY)
    dma = pltpu.SemaphoreType.DMA
    args = (
        alignment, gain.reshape(1, -1), shift.reshape(1, -1), wl.T, bl.reshape(1, -1),
        wr.T, br.reshape(1, -1), ow, ob.reshape(1, -1),
    )
    scratch = [pltpu.VMEM(a.shape, a.dtype) for a in args]
    scratch += [
        pltpu.VMEM((8, 16, 128), BF16),
        pltpu.VMEM((4, 16, 128), BF16),
        pltpu.VMEM((64, 128), BF16),
        pltpu.VMEM((8, 16, 128), BF16),
        pltpu.VMEM((8, 16, 128), BF16),
        pltpu.VMEM((8, 64, 128), BF16),
        pltpu.VMEM((2, 16, 512), BF16),
        pltpu.VMEM((4, 16, 256), BF16),
        pltpu.VMEM((4, 4, 16, 256), BF16),
        pltpu.VMEM((4, 8, 16, 512), BF16),
        pltpu.VMEM((8, 4, 16, 256), BF16),
        pltpu.VMEM((4, 4, 16, 256), BF16),
        pltpu.VMEM((8, 4, 16, 256), BF16),
        pltpu.VMEM((256, 1024), BF16),
        pltpu.VMEM((128, 128), F32),
        pltpu.VMEM((128, 128), F32),
        pltpu.VMEM((128, 128), F32),
        dma((len(args),)),
    ]
    for n in (7, 4, 3, 3, 7, 7, 3, 3, 7, 3, 7, 1):
        scratch += [dma((n,)), dma((n,))]
    args = tuple(pltpu.with_memory_space_constraint(a, pltpu.HBM) for a in args)
    return pl.pallas_call(
        kernel,
        out_shape=jax.ShapeDtypeStruct((8, 16, 128), BF16),
        in_specs=[any_space] * len(args),
        out_specs=pl.BlockSpec(memory_space=pltpu.VMEM),
        scratch_shapes=scratch,
        compiler_params=pltpu.CompilerParams(
            collective_id=0, has_side_effects=True, vmem_limit_bytes=32 << 20
        ),
    )(*args)


def solution(mesh):
    in_specs = (P(("seq", "res"), None, None), P(), P(), P(), P(), P(), P(), P(), P())
    return jax.shard_map(
        body, mesh=mesh, in_specs=in_specs, out_specs=P("res", "seq", None), check_vma=False
    )
```
